32 devices in a mesh: seq: 8 (over z, y), mp: 4 (over x, core).
Axes of the slice: x: 2, y: 2, z: 4, core: 2. Of those that a mesh axis runs over, the one named last changes fastest.
Arguments:
- latents: bfloat16 [2048, 1536], P('seq'), may hold values from -6 to 6
- w_query: bfloat16 [1536, 1536], P(None, 'mp'), may hold values from -0.15625 to 0.15625
- w_key: bfloat16 [1536, 1536], P(None, 'mp'), may hold values from -0.15625 to 0.15625
- w_value: bfloat16 [1536, 1536], P(None, 'mp'), may hold values from -0.15625 to 0.15625
- w_out: bfloat16 [1536, 1536], P('mp'), may hold values from -0.15625 to 0.15625
- head_gain: float32 [1536], P('mp'), may hold values from 0.25 to 1.75
- grad_out: bfloat16 [2048, 1536], P('seq', 'mp'), may hold values from -6 to 6
Outputs:
- branch: bfloat16 [2048, 1536], P('seq', 'mp')
- d_latents: bfloat16 [2048, 1536], P('seq', 'mp')
The draws below stay inside these ranges and needn't reach their ends.
All inputs are finite; a program needn't handle non-finite values.
Results may differ from the reference program's by a relative error of at most 0.013.
Values may be sent and summed in bfloat16 or wider, within the bound.
A program may use at most 64 MiB of HBM per device.

```python
import jax
import jax.numpy as jnp
from jax import lax

D = 1536
HEADS = 24
HD = 64
LENGTH = 2048
N_MP = 4


def shard_levels(stream_key, dims, shards, least, high):
    level, own = 1.0, jax.random.fold_in(stream_key, 6)
    for position, shards_of in shards:
        heights = jnp.exp(jax.random.uniform(jax.random.fold_in(own, position), (shards_of,), jnp.float32, least / len(shards), high / len(shards)))
        level = level * jnp.repeat(heights, dims[position] // shards_of).reshape([-1 if axis == position else 1 for axis in range(len(dims))])
    return level


def gaussian(key, dims, scale, most, split=(), kind=jnp.bfloat16):
    values = scale * jax.random.normal(key, dims, jnp.float32)
    if split:
        values = values * shard_levels(key, dims, split, -0.22, 0.18)
    return jnp.clip(values, -most, most).astype(kind)


def setup_inputs(seed: int = 0) -> dict:
    key_of = jax.random.split(jax.random.key(seed), 8)
    latents = gaussian(key_of[0], (LENGTH, D), 1.0, 6.0, ((0, 8),))
    w_query = gaussian(key_of[1], (D, D), D ** -0.5, 0.15625, ((1, 4),))
    w_key = gaussian(key_of[2], (D, D), D ** -0.5, 0.15625, ((1, 4),))
    w_value = gaussian(key_of[3], (D, D), D ** -0.5, 0.15625, ((1, 4),))
    w_out = gaussian(key_of[4], (D, D), D ** -0.5, 0.15625, ((0, 4),))
    head_gain = jnp.clip(1.0 + 0.15 * jax.random.normal(key_of[5], (D,), jnp.float32), 0.25, 1.75)
    grad_out = gaussian(key_of[6], (LENGTH, D), 1.0, 6.0, ((0, 8), (1, 4)))
    return dict(latents=latents, w_query=w_query, w_key=w_key, w_value=w_value, w_out=w_out, head_gain=head_gain, grad_out=grad_out)


highest_precision = lax.Precision.HIGHEST
epsilon = 1e-06

def feature_map(inputs):
    return jnp.where(inputs > 0, inputs + 1.0, jnp.exp(jnp.minimum(inputs, 0.0)))

def feature_slope(inputs):
    return jnp.where(inputs > 0, jnp.ones_like(inputs), jnp.exp(jnp.minimum(inputs, 0.0)))

def causal_table(block_rows):
    return (jnp.arange(block_rows)[:, None] >= jnp.arange(block_rows)[None, :]).astype(jnp.float32)

def reference(latents, w_query, w_key, w_value, w_out, head_gain, grad_out):
    total_rows = latents.shape[0]
    query_raw = jnp.dot(latents, w_query, preferred_element_type=jnp.float32).reshape(total_rows, HEADS, HD)
    key_raw = jnp.dot(latents, w_key, preferred_element_type=jnp.float32).reshape(total_rows, HEADS, HD)
    value_matrix = jnp.dot(latents, w_value, preferred_element_type=jnp.float32).reshape(total_rows, HEADS, HD)
    mapped_query = feature_map(query_raw)
    mapped_key = feature_map(key_raw)
    block_rows = min(512, total_rows)
    block_count = total_rows // block_rows
    causal_mask = causal_table(block_rows)

    def blocked(array):
        return array.reshape(block_count, block_rows, HEADS, HD)

    def forward_step(running_state, inputs):
        mapped_query_block, mapped_key_block, value_block = inputs
        score_matrix = jnp.einsum('thk,shk->hts', mapped_query_block, mapped_key_block, precision=highest_precision) * causal_mask
        unnormed_block = jnp.einsum('hts,shv->thv', score_matrix, value_block, precision=highest_precision)
        unnormed_block = unnormed_block + jnp.einsum('lsd,sdq->lsq', mapped_query_block, running_state, precision=highest_precision)
        updated_state = running_state + jnp.einsum('omw,omd->mwd', mapped_key_block, value_block, precision=highest_precision)
        return (updated_state, (unnormed_block, running_state))
    initial = jnp.zeros((HEADS, HD, HD), jnp.float32)
    _, (raw_blocks, befores) = lax.scan(forward_step, initial, (blocked(mapped_query), blocked(mapped_key), blocked(value_matrix)))
    raw = raw_blocks.reshape(total_rows, HEADS, HD)
    inv_scale = lax.rsqrt(lax.optimization_barrier(jnp.mean(raw * raw, axis=-1, keepdims=True)) + epsilon)
    gain_rows = head_gain.reshape(HEADS, HD)
    attn = (raw * inv_scale * gain_rows).astype(jnp.bfloat16).reshape(total_rows, D)
    group_width = D // N_MP
    summed = jnp.zeros((total_rows, D), jnp.float32)
    for group in range(N_MP):
        lower = group * group_width
        partial_out = jnp.dot(attn[:, lower:lower + group_width], w_out[lower:lower + group_width], preferred_element_type=jnp.float32)
        summed = summed + lax.optimization_barrier(partial_out.astype(jnp.bfloat16)).astype(jnp.float32)
    branch = summed.astype(jnp.bfloat16)
    contract = (((1,), (1,)), ((), ()))
    d_attn = lax.dot_general(grad_out, w_out, contract, preferred_element_type=jnp.float32).reshape(total_rows, HEADS, HD)
    upstream = d_attn * gain_rows
    row_stat = lax.optimization_barrier(jnp.mean(raw * upstream, axis=-1, keepdims=True))
    unnormed_gradient = inv_scale * upstream - inv_scale * inv_scale * inv_scale * raw * row_stat

    def backward_step(running_state, inputs):
        mapped_query_block, mapped_key_block, value_block, unnormed_block_gradient, prior_state_sum = inputs
        score_matrix = jnp.einsum('thk,shk->hts', mapped_query_block, mapped_key_block, precision=highest_precision) * causal_mask
        mixed_output = jnp.einsum('thv,shv->hts', unnormed_block_gradient, value_block, precision=highest_precision) * causal_mask
        feature_query_gradient = jnp.einsum('fui,ifc->ufc', mixed_output, mapped_key_block, precision=highest_precision) + jnp.einsum('pue,ure->pur', unnormed_block_gradient, prior_state_sum, precision=highest_precision)
        feature_key_gradient = jnp.einsum('xbc,bxj->cxj', mixed_output, mapped_query_block, precision=highest_precision) + jnp.einsum('wqj,qtj->wqt', value_block, running_state, precision=highest_precision)
        value_gradient = jnp.einsum('fud,ufx->dfx', score_matrix, unnormed_block_gradient, precision=highest_precision) + jnp.einsum('eul,ulw->euw', mapped_key_block, running_state, precision=highest_precision)
        updated_state = running_state + jnp.einsum('wei,wej->eij', mapped_query_block, unnormed_block_gradient, precision=highest_precision)
        return (updated_state, (feature_query_gradient, feature_key_gradient, value_gradient))
    _, (feature_query_gradient, feature_key_gradient, value_gradient) = lax.scan(backward_step, initial, (blocked(mapped_query), blocked(mapped_key), blocked(value_matrix), blocked(unnormed_gradient), befores), reverse=True)
    d_query = (feature_query_gradient.reshape(total_rows, HEADS, HD) * feature_slope(query_raw)).astype(jnp.bfloat16).reshape(total_rows, D)
    d_key = (feature_key_gradient.reshape(total_rows, HEADS, HD) * feature_slope(key_raw)).astype(jnp.bfloat16).reshape(total_rows, D)
    d_value = value_gradient.reshape(total_rows, D).astype(jnp.bfloat16)
    summed_in = jnp.zeros((total_rows, D), jnp.float32)
    for group in range(N_MP):
        lower = group * group_width
        upper = lower + group_width
        partial_in = lax.dot_general(d_query[:, lower:upper], w_query[:, lower:upper], contract, preferred_element_type=jnp.float32)
        partial_in = partial_in + lax.dot_general(d_key[:, lower:upper], w_key[:, lower:upper], contract, preferred_element_type=jnp.float32)
        partial_in = partial_in + lax.dot_general(d_value[:, lower:upper], w_value[:, lower:upper], contract, preferred_element_type=jnp.float32)
        summed_in = summed_in + lax.optimization_barrier(partial_in.astype(jnp.bfloat16)).astype(jnp.float32)
    d_latents = summed_in.astype(jnp.bfloat16)
    return (branch, d_latents)
```

```python
import functools

import jax
import jax.numpy as jnp
from jax import lax
from jax.experimental import pallas as pl
from jax.experimental.pallas import tpu as pltpu
from jax.sharding import PartitionSpec as P

HD = 64
PAIR = 2 * HD
EPS = 1e-06
MESH = pl.DeviceIdType.MESH
F32 = jnp.float32
BF16 = jnp.bfloat16


def mm(a, b):
    return jnp.dot(a, b, preferred_element_type=F32)


def mm_nt(a, b):
    return lax.dot_general(a, b, (((1,), (1,)), ((), ())), preferred_element_type=F32)


def mm_tn(a, b):
    return lax.dot_general(a, b, (((0,), (0,)), ((), ())), preferred_element_type=F32)


def phi(u):
    return jnp.where(u > 0, u + 1.0, jnp.exp(jnp.minimum(u, 0.0)))


def kernel(
    S, lat_h, wq_h, wk_h, wv_h, wo_h, gain_ref, go_h, branch_ref, dlat_ref,
    lat, wall, wo, gfull, fq, fk, vb, sct, raw, dat, drb, dfq, dqkv, kl, vl,
    own, st, prc, psum, gath, tx, rx, acc,
    loc, gs, gr, ps, pr, zs, zr, rs_s, rs_r,
):
    R, D = lat.shape
    W = wo.shape[0]
    NP = W // PAIR
    Z = S // 2
    seq = lax.axis_index("seq")
    mp = lax.axis_index("mp")
    z, y = seq // 2, seq % 2
    pair = z * 2 + (1 - y)
    half, core = mp // 2, mp % 2
    sib = half * 2 + (1 - core)
    xp = (1 - half) * 2 + core
    diag = (1 - half) * 2 + (1 - core)

    def cols(m):
        return pl.ds(pl.multiple_of(m * W, 128), W)

    def local(src, dst, i):
        return pltpu.make_async_copy(src, dst, loc.at[i])

    c_lat = local(lat_h, lat, 0)
    c_wk = local(wk_h, wall.at[:, 0:W], 1)
    c_wv = local(wv_h, wall.at[:, W : 2 * W], 2)
    c_wq = local(wq_h, wall.at[:, 2 * W : 3 * W], 3)
    c_wo = local(wo_h, wo, 4)
    c_go = local(go_h, gfull.at[:, cols(mp)], 5)
    for c in (c_lat, c_wk, c_wv, c_wq, c_go, c_wo):
        c.start()

    barrier = pltpu.get_barrier_semaphore()

    def greet(where):
        pl.semaphore_signal(barrier, inc=1, device_id=where, device_id_type=MESH)

    greet({"mp": sib})
    greet({"mp": xp})
    greet({"seq": pair})

    def line(k, carry):
        other = lax.rem(z + 1 + k, Z)
        greet({"seq": other * 2 + y})
        return carry

    lax.fori_loop(0, Z - 1, line, 0)
    pl.semaphore_wait(barrier, 2 + Z)

    def remote(src, dst, s, r, where):
        return pltpu.make_async_remote_copy(
            src_ref=src, dst_ref=dst, send_sem=s, recv_sem=r, device_id=where, device_id_type=MESH
        )

    g_x = remote(go_h, gfull.at[:, cols(mp)], gs.at[0], gr.at[0], {"mp": xp})
    g_s = remote(go_h, gfull.at[:, cols(mp)], gs.at[1], gr.at[1], {"mp": sib})
    g_f = remote(gfull.at[:, cols(xp)], gfull.at[:, cols(xp)], gs.at[2], gr.at[2], {"mp": sib})
    g_x.start()
    g_s.start()

    lane = lax.broadcasted_iota(jnp.int32, (1, PAIR), 1)
    low = lane < HD

    def split(a):
        zero = jnp.zeros_like(a)
        return jnp.concatenate([jnp.where(low, a, zero), jnp.where(low, zero, a)], axis=0)

    def squeeze(a):
        return jnp.where(low, a[:HD], a[HD:])

    def pc(p):
        return slice(p * PAIR, (p + 1) * PAIR)

    def pr_(p):
        return slice(p * HD, (p + 1) * HD)

    def p_copy(e):
        return remote(st.at[e], prc.at[e], ps.at[e], pr.at[e], {"seq": pair})

    def z_copy(e, slot, to):
        return remote(
            psum.at[e], gath.at[e, slot], zs.at[e, to], zr.at[e, slot], {"seq": to * 2 + y}
        )

    def z_range(e, sending):
        up = (e == 0) == sending
        return (z + 1, Z) if up else (0, z)

    def z_send(e):
        p_copy(e).wait_recv()
        psum[e] = (own[e] + prc[e].astype(F32)).astype(BF16)
        lo, hi = z_range(e, True)

        def body(k, carry):
            z_copy(e, z, k).start()
            return carry

        lax.fori_loop(lo, hi, body, 0)

    def z_total(e):
        lo, hi = z_range(e, False)
        first = (y == 1) if e == 0 else (y == 0)
        start = jnp.where(first, prc[e].astype(F32), 0.0)

        def body(k, carry):
            z_copy(e, k, k).wait_recv()
            return carry + gath[e, k].astype(F32)

        return lax.fori_loop(lo, hi, body, start).astype(BF16)

    def z_drain(e):
        p_copy(e).wait_send()
        lo, hi = z_range(e, True)

        def body(k, carry):
            z_copy(e, z, k).wait_send()
            return carry

        lax.fori_loop(lo, hi, body, 0)

    c_lat.wait()
    c_wk.wait()
    x = lat[...]
    fk[...] = phi(mm(x, wall[:, 0:W]))
    c_wv.wait()
    vb[...] = mm(x, wall[:, W : 2 * W]).astype(BF16)
    for p in range(NP):
        s = squeeze(mm_tn(fk[:, pc(p)].astype(BF16), vb[:, pc(p)]))
        own[0, pr_(p)] = s
        st[0, pr_(p)] = s.astype(BF16)
    p_copy(0).start()

    c_wq.wait()
    fq[...] = phi(mm(x, wall[:, 2 * W : 3 * W]))
    z_send(0)
    g_x.wait_recv()
    c_go.wait()
    g_f.start()

    t_row = lax.broadcasted_iota(jnp.int32, (R, 2 * R), 0)
    s_col = lax.rem(lax.broadcasted_iota(jnp.int32, (R, 2 * R), 1), R)
    lower = t_row >= s_col
    upper = t_row <= s_col

    for p in range(NP):
        q = fq[:, pc(p)].astype(BF16)
        k = fk[:, pc(p)].astype(BF16)
        score = jnp.where(lower, mm_nt(q, split(k)), 0.0).astype(BF16)
        raw[:, pc(p)] = mm(score, split(vb[:, pc(p)]))
        sct[p] = jnp.where(upper, mm_nt(k, split(q)), 0.0).astype(BF16)

    c_wo.wait()
    g_s.wait_recv()
    g_f.wait_recv()
    gain = gain_ref[...]
    dat[...] = mm_nt(gfull[...], wo[...]) * gain

    ones = jnp.where(
        (lax.broadcasted_iota(jnp.int32, (PAIR, PAIR), 0) < HD)
        == (lax.broadcasted_iota(jnp.int32, (PAIR, PAIR), 1) < HD),
        1.0 / HD,
        0.0,
    ).astype(BF16)

    prefix = z_total(0)
    attn = []
    for p in range(NP):
        q = fq[:, pc(p)].astype(BF16)
        r = raw[:, pc(p)] + mm(q, split(prefix[pr_(p)]))
        inv = lax.rsqrt(mm((r * r).astype(BF16), ones) + EPS)
        rn = r * inv
        attn.append((rn * gain[:, pc(p)]).astype(BF16))
        up = dat[:, pc(p)]
        stat = mm((rn * up).astype(BF16), ones)
        d = (inv * (up - rn * stat)).astype(BF16)
        drb[:, pc(p)] = d
        s = squeeze(mm_tn(q, d))
        own[1, pr_(p)] = s
        st[1, pr_(p)] = s.astype(BF16)
    p_copy(1).start()
    attn = jnp.concatenate(attn, axis=1)

    def r_copy(e, i, where):
        return remote(tx.at[e, i], rx.at[e, i], rs_s.at[e, i], rs_r.at[e, i], {"mp": where})

    def scatter_first(e, part):
        tx[e, 0] = part(diag).astype(BF16)
        r_copy(e, 0, sib).start()

    def scatter_rest(e, part):
        mine = part(xp)
        r_copy(e, 0, sib).wait_recv()
        tx[e, 1] = (mine + rx[e, 0].astype(F32)).astype(BF16)
        r_copy(e, 1, xp).start()
        tx[e, 2] = part(sib).astype(BF16)
        r_copy(e, 2, sib).start()
        acc[e] = part(mp)

    def scatter_end(e, out):
        r_copy(e, 2, sib).wait_recv()
        r_copy(e, 1, xp).wait_recv()
        out[...] = (acc[e] + rx[e, 1].astype(F32) + rx[e, 2].astype(F32)).astype(BF16)
        for i in range(3):
            r_copy(e, i, sib).wait_send()

    def out_part(m):
        return mm(attn, wo[:, cols(m)])

    scatter_first(0, out_part)
    z_send(1)
    scatter_rest(0, out_part)

    for p in range(NP):
        q = fq[:, pc(p)].astype(BF16)
        k = fk[:, pc(p)].astype(BF16)
        v = vb[:, pc(p)]
        d = drb[:, pc(p)]
        d2 = split(d)
        mixed = jnp.where(lower, mm_nt(d, split(v)), 0.0).astype(BF16)
        g = mm(mixed, split(k)) + mm_nt(d, split(prefix[pr_(p)]))
        dqkv[:, 2 * W + p * PAIR : 2 * W + (p + 1) * PAIR] = (
            g * jnp.minimum(fq[:, pc(p)], 1.0)
        ).astype(BF16)
        mixed_t = jnp.where(upper, mm_nt(v, d2), 0.0).astype(BF16)
        kl[:, pc(p)] = mm(mixed_t, split(q))
        vl[:, pc(p)] = mm(sct[p], d2)

    suffix = z_total(1)
    for p in range(NP):
        f = fk[:, pc(p)]
        bd = split(suffix[pr_(p)])
        g = kl[:, pc(p)] + mm_nt(vb[:, pc(p)], bd)
        dqkv[:, pc(p)] = (g * jnp.minimum(f, 1.0)).astype(BF16)
        dqkv[:, W + p * PAIR : W + (p + 1) * PAIR] = (
            vl[:, pc(p)] + mm(f.astype(BF16), bd)
        ).astype(BF16)

    dx = dqkv[...]

    def in_part(m):
        return mm_nt(dx, wall[cols(m), :])

    scatter_first(1, in_part)
    scatter_rest(1, in_part)
    scatter_end(0, branch_ref)
    scatter_end(1, dlat_ref)

    g_x.wait_send()
    g_s.wait_send()
    g_f.wait_send()
    z_drain(0)
    z_drain(1)


def per_device(S, latents, w_query, w_key, w_value, w_out, head_gain, grad_out):
    R, D = latents.shape
    W = w_query.shape[1]
    NP = W // PAIR
    NS = NP * HD
    Z = S // 2
    hbm = pl.BlockSpec(memory_space=pl.ANY)
    vmem = pl.BlockSpec(memory_space=pltpu.VMEM)
    V = pltpu.VMEM
    dma = pltpu.SemaphoreType.DMA
    out = jax.ShapeDtypeStruct((R, W), BF16)
    return pl.pallas_call(
        functools.partial(kernel, S),
        out_shape=(out, out),
        in_specs=[hbm, hbm, hbm, hbm, hbm, vmem, hbm],
        out_specs=(vmem, vmem),
        scratch_shapes=[
            V((R, D), BF16),
            V((D, 3 * W), BF16),
            V((W, D), BF16),
            V((R, D), BF16),
            V((R, W), F32),
            V((R, W), F32),
            V((R, W), BF16),
            V((NP, R, 2 * R), BF16),
            V((R, W), F32),
            V((R, W), F32),
            V((R, W), BF16),
            V((R, W), F32),
            V((R, 3 * W), BF16),
            V((R, W), F32),
            V((R, W), F32),
            V((2, NS, PAIR), F32),
            V((2, NS, PAIR), BF16),
            V((2, NS, PAIR), BF16),
            V((2, NS, PAIR), BF16),
            V((2, Z, NS, PAIR), BF16),
            V((2, 3, R, W), BF16),
            V((2, 3, R, W), BF16),
            V((2, R, W), F32),
            dma((6,)),
            dma((3,)),
            dma((3,)),
            dma((2,)),
            dma((2,)),
            dma((2, Z)),
            dma((2, Z)),
            dma((2, 3)),
            dma((2, 3)),
        ],
        compiler_params=pltpu.CompilerParams(
            collective_id=0, has_side_effects=True, vmem_limit_bytes=48 * 1024 * 1024
        ),
    )(latents, w_query, w_key, w_value, w_out, head_gain.reshape(1, W), grad_out)


def solution(mesh):
    in_specs = (
        P("seq", None),
        P(None, "mp"),
        P(None, "mp"),
        P(None, "mp"),
        P("mp", None),
        P("mp"),
        P("seq", "mp"),
    )
    out_specs = (P("seq", "mp"), P("seq", "mp"))
    return jax.shard_map(
        functools.partial(per_device, mesh.shape["seq"]),
        mesh=mesh,
        in_specs=in_specs,
        out_specs=out_specs,
        check_vma=False,
    )
```
